32 devices in a mesh: req: 8 (over z, x), seq: 4 (over y, core).
Axes of the slice: x: 2, y: 2, z: 4, core: 2. Of those that a mesh axis runs over, the one named last changes fastest.
Arguments:
- x_in: bfloat16 [16384, 2560], P(('req', 'seq')), may hold values from -6 to 6
- bc_in: bfloat16 [16384, 256], P(('req', 'seq')), may hold values from -6 to 6
- z_in: bfloat16 [16384, 2560], P(('req', 'seq')), may hold values from -6 to 6
- dt_raw: bfloat16 [16384, 40], P(('req', 'seq')), may hold values from -3 to 22
- conv_weight: float32 [4, 2816], replicated, may hold values from -3 to 3
- conv_bias: float32 [2816], replicated, may hold values from -0.5 to 0.5
- dt_bias: float32 [40], replicated, may hold values from -5 to -4
- a_log: float32 [40], replicated, may hold values from -3.95 to 1.17
- d_skip: float32 [40], replicated, may hold values from 0.5 to 2
- norm_gain: float32 [2560], replicated, may hold values from 0.1 to 1.9
- w_out: bfloat16 [2560, 2560], replicated, may hold values from -0.125 to 0.125
- prompt_stretches: int32 [16], replicated, may hold values from 1 to 16, as said below
Outputs:
- mixed_out: bfloat16 [16384, 2560], P(('req', 'seq'))
- end_states: float32 [64, 40, 64, 128], P('req', 'seq')
The draws below stay inside these ranges and needn't reach their ends.
Inputs may be any that keep to these rules, and one draw needn't show every extreme that they name: `prompt_stretches`: the lengths sum to 64; the last prompt is exactly 16 stretches long and none is longer.
All inputs are finite; a program needn't handle non-finite values.
Results may differ from the reference program's by a relative error of at most 0.0073.
Values may be sent and summed in bfloat16 or wider, within the bound.
A program may use at most 448 MiB of HBM per device.

```python
import math
import jax
import jax.numpy as jnp
from jax import lax

D = 2560
H = 40
N = 128
KCONV = 4
STRETCH = 256
LMAX_CH = 16
TOK_DEV = 512
DI = 2560
TOKEN_TOTAL = 16384
STRETCHES = 64
REQS = 16
N_REQ = 8
N_SEQ = 4


def draw_dt_raw(key, part):
    base_random_key, flurry_random_key, height_random_key = jax.random.split(key, 3)
    base_value_rows = jnp.clip(0.5 * jax.random.normal(base_random_key, (TOKEN_TOTAL, H), jnp.float32), -3.0, 3.0)
    flurry_lengths = jax.random.uniform(flurry_random_key, (TOKEN_TOTAL, 1), jnp.float32) < 1.0 / 1024.0
    column_height = jax.random.uniform(height_random_key, (TOKEN_TOTAL, 1), jnp.float32, 17.0, 22.0)
    return jnp.where(flurry_lengths, column_height, base_value_rows).astype(jnp.bfloat16)


def draw_a_log(key, part):
    pick_key, slow_key, fast_key = jax.random.split(key, 3)
    fast_share = 0.5
    is_fast = jax.random.uniform(pick_key, (H,), jnp.float32) < fast_share
    slow_rate = jnp.exp(jax.random.uniform(slow_key, (H,), jnp.float32, math.log(0.02), math.log(0.04)))
    fast_rate = jnp.exp(jax.random.uniform(fast_key, (H,), jnp.float32, math.log(1.8), math.log(3.2)))
    return jnp.log(jnp.where(is_fast, fast_rate, slow_rate))


def draw_prompt_stretches(key, part):
    level_key, noise_key = jax.random.split(jax.random.fold_in(key, 7), 2)
    others = REQS - 1
    room = LMAX_CH - 1
    extra = STRETCHES - LMAX_CH - others
    level = jax.random.randint(level_key, (others,), 0, 16, jnp.int32)
    favour = level * level
    noise = jax.random.randint(noise_key, (others, room), 0, 256, jnp.int32)
    slot_ids = jnp.arange(others * room, dtype=jnp.int32).reshape(others, room)
    scores = (favour[:, None] + noise) * (others * room) + slot_ids
    order = jnp.argsort(-scores.reshape(-1), stable=True).astype(jnp.int32)
    ranks = jnp.argsort(order, stable=True).astype(jnp.int32).reshape(others, room)
    taken = (ranks < extra).astype(jnp.int32)
    lengths = 1 + jnp.sum(taken, axis=1).astype(jnp.int32)
    return jnp.concatenate([lengths, jnp.full((1,), LMAX_CH, jnp.int32)]).astype(jnp.int32)


def steps_of(stream_key, shape, pieces, low, largest):
    level, own = 1.0, jax.random.fold_in(stream_key, 6)
    for dim, parts in pieces:
        heights = jnp.exp(jax.random.uniform(jax.random.fold_in(own, dim), (parts,), jnp.float32, low / len(pieces), largest / len(pieces)))
        level = level * jnp.repeat(heights, shape[dim] // parts).reshape([-1 if axis == dim else 1 for axis in range(len(shape))])
    return level


def gaussian(key, dims, spread, most, cuts=(), kind=jnp.bfloat16):
    factor_of = steps_of(key, dims, cuts, -0.22, 0.18) if cuts else 1.0
    values = jax.random.normal(key, dims, jnp.float32) * spread * factor_of
    return jnp.minimum(jnp.maximum(values, -most), most).astype(kind)


def setup_inputs(seed: int = 0) -> dict:
    streams_of = jax.random.split(jax.random.key(seed), 13)
    return {
        "x_in": gaussian(streams_of[0], (TOKEN_TOTAL, DI), 1.0, 6.0, ((0, 32),)),
        "bc_in": gaussian(streams_of[1], (TOKEN_TOTAL, 2 * N), 1.0, 6.0, ((0, 32),)),
        "z_in": gaussian(streams_of[2], (TOKEN_TOTAL, DI), 1.0, 6.0, ((0, 32),)),
        "dt_raw": draw_dt_raw(jax.random.fold_in(streams_of[12], 71), 0),
        "conv_weight": gaussian(streams_of[4], (KCONV, DI + 2 * N), KCONV ** -0.5, 3.0, (), jnp.float32),
        "conv_bias": jnp.clip(jax.random.uniform(streams_of[5], (DI + 2 * N,), jnp.float32, -0.5, 0.5), -0.5, 0.5),
        "dt_bias": jnp.clip(jax.random.uniform(streams_of[6], (H,), jnp.float32, -5.0, -4.0), -5.0, -4.0),
        "a_log": draw_a_log(jax.random.fold_in(streams_of[12], 71), 0),
        "d_skip": jnp.clip(jax.random.uniform(streams_of[8], (H,), jnp.float32, 0.5, 2.0), 0.5, 2.0),
        "norm_gain": jnp.clip(1.0 + 0.18 * jax.random.normal(streams_of[9], (DI,), jnp.float32), 0.1, 1.9),
        "w_out": gaussian(streams_of[10], (DI, D), DI ** -0.5, 0.125),
        "prompt_stretches": draw_prompt_stretches(jax.random.fold_in(streams_of[12], 71), 0),
    }


def reorder_rows(token_rows):
    blocks = token_rows.reshape(N_REQ, N_SEQ, N_REQ, TOK_DEV // N_REQ, -1)
    return blocks.transpose(2, 1, 0, 3, 4).reshape(TOKEN_TOTAL, -1)

def stretch_flags(prompt_stretches, stretch_ids):
    lengths = prompt_stretches.astype(jnp.int32)
    firsts = (jnp.cumsum(lengths) - lengths).astype(jnp.int32)
    last_stretches = (firsts + lengths - 1).astype(jnp.int32)
    starts = jnp.any(stretch_ids[:, None] == firsts[None, :], axis=1)
    finals = jnp.any(stretch_ids[:, None] == last_stretches[None, :], axis=1)
    return (starts, finals)

def conv_stretch(row_block, history, weight, conv_bias):
    conv_span = weight.shape[0]
    length = row_block.shape[0]
    extended = jnp.concatenate([history, row_block], axis=0).astype(jnp.float32)
    running = conv_bias[None, :]
    for offset in range(conv_span):
        running = running + weight[offset][None, :] * extended[offset:offset + length]
    return jax.nn.silu(running).astype(jnp.bfloat16)

def local_stretch(x_stretch, bc_stretch, dt_stretch, dt_bias, a_log):
    state_size = bc_stretch.shape[1] // 2
    b_mat = bc_stretch[:, :state_size]
    c_mat = bc_stretch[:, state_size:]
    step_size = jax.nn.softplus(dt_stretch.astype(jnp.float32) + dt_bias[None, :])
    log_decay = jnp.cumsum(-jnp.exp(a_log)[None, :] * step_size, axis=0)
    scores = jnp.dot(c_mat, b_mat.T, preferred_element_type=jnp.float32)
    stretch_len = scores.shape[0]
    causal = jnp.arange(stretch_len)[:, None] >= jnp.arange(stretch_len)[None, :]
    by_head = log_decay.T
    segment = by_head[:, :, None] - by_head[:, None, :]
    decay_mask = jnp.where(causal[None], jnp.exp(jnp.where(causal[None], segment, 0.0)), 0.0)
    mixing = (scores[None] * decay_mask * step_size.T[:, None, :]).astype(jnp.bfloat16)
    y_diag = jnp.einsum('htu,uhp->thp', mixing.astype(jnp.float32), x_stretch.astype(jnp.float32))
    tail_weight = jnp.exp(log_decay[-1][None, :] - log_decay) * step_size
    weighted_x = (x_stretch.astype(jnp.float32) * tail_weight[:, :, None]).astype(jnp.bfloat16)
    stretch_state = jnp.einsum('uhp,un->hpn', weighted_x.astype(jnp.float32), b_mat.astype(jnp.float32), precision=lax.Precision.HIGHEST)
    return (y_diag, stretch_state, log_decay)

def finish_stretch(y_diag, log_decay, state_in, x_stretch, c_mat, z_stretch, d_skip, norm_gain):
    state_low = state_in.astype(jnp.bfloat16)
    y_off = jnp.exp(log_decay)[:, :, None] * jnp.einsum('tn,hpn->thp', c_mat.astype(jnp.float32), state_low.astype(jnp.float32), precision=lax.Precision.HIGHEST)
    mixed_rows = y_diag + y_off + d_skip[None, :, None] * x_stretch.astype(jnp.float32)
    mixed_rows = mixed_rows.reshape(mixed_rows.shape[0], -1)
    gated_rows = mixed_rows * jax.nn.silu(z_stretch.astype(jnp.float32))
    inv_rms = lax.rsqrt(lax.optimization_barrier(jnp.mean(gated_rows * gated_rows, axis=-1, keepdims=True)) + 1e-05)
    return (gated_rows * inv_rms * norm_gain[None, :]).astype(jnp.bfloat16)

def reference(x_in, bc_in, z_in, dt_raw, conv_weight, conv_bias, dt_bias, a_log, d_skip, norm_gain, w_out, prompt_stretches):
    inner_width = x_in.shape[1]
    head_count = a_log.shape[0]
    head_dim = inner_width // head_count
    conv_span = conv_weight.shape[0]
    x_rows = reorder_rows(x_in).reshape(STRETCHES, STRETCH, inner_width)
    bc_rows = reorder_rows(bc_in).reshape(STRETCHES, STRETCH, 2 * N)
    z_rows = reorder_rows(z_in).reshape(STRETCHES, STRETCH, inner_width)
    dt_rows = reorder_rows(dt_raw).reshape(STRETCHES, STRETCH, head_count)
    starts, finals = stretch_flags(prompt_stretches, jnp.arange(STRETCHES, dtype=jnp.int32))

    def advance(carried, element):
        state_now, hist_x, hist_bc = carried
        x_stretch, bc_stretch, z_stretch, dt_stretch, is_start, is_final = element
        hist_x = jnp.where(is_start, jnp.zeros_like(hist_x), hist_x)
        hist_bc = jnp.where(is_start, jnp.zeros_like(hist_bc), hist_bc)
        conv_x = conv_stretch(x_stretch, hist_x, conv_weight[:, :inner_width], conv_bias[:inner_width])
        conv_bc = conv_stretch(bc_stretch, hist_bc, conv_weight[:, inner_width:], conv_bias[inner_width:])
        x_heads = conv_x.reshape(STRETCH, head_count, head_dim)
        y_diag, stretch_state, log_decay = local_stretch(x_heads, conv_bc, dt_stretch, dt_bias, a_log)
        state_in = jnp.where(is_start, jnp.zeros_like(state_now), state_now)
        normed = finish_stretch(y_diag, log_decay, state_in, x_heads, conv_bc[:, N:], z_stretch, d_skip, norm_gain)
        projected = jnp.dot(normed, w_out, preferred_element_type=jnp.float32).astype(jnp.bfloat16)
        state_out = jnp.exp(log_decay[-1])[:, None, None] * state_in + stretch_state
        ending = jnp.where(is_final, state_out, jnp.zeros_like(state_out))
        return ((state_out, x_stretch[STRETCH - conv_span + 1:], bc_stretch[STRETCH - conv_span + 1:]), (projected, ending))
    initial = (jnp.zeros((head_count, head_dim, N), jnp.float32), jnp.zeros((conv_span - 1, inner_width), jnp.bfloat16), jnp.zeros((conv_span - 1, 2 * N), jnp.bfloat16))
    final_carry, outputs = lax.scan(advance, initial, (x_rows, bc_rows, z_rows, dt_rows, starts, finals))
    projected, endings = outputs
    mixed_out = reorder_rows(projected.reshape(TOKEN_TOTAL, -1))
    return (mixed_out, endings)
```

```python
import math

import jax
import jax.numpy as jnp
from jax import lax
from jax.experimental import pallas as pl
from jax.experimental.pallas import tpu as pltpu
from jax.sharding import PartitionSpec as P

N = 128
STRETCH = 256
LMAX_CH = 16
HEADS = 4
WIDTH = 256
HIST = 8
LOG2E = math.log2(math.e)


def conv_kernel(rows_ref, hist_ref, weight_ref, bias_ref, tail_ref, conv_ref, state_ref, b_mat):
    span = weight_ref.shape[0]
    extended = jnp.concatenate(
        [hist_ref[0].astype(jnp.float32), rows_ref[0].astype(jnp.float32)], axis=0
    )
    running = bias_ref[...]
    for offset in range(span):
        first = HIST - (span - 1) + offset
        running = running + weight_ref[offset : offset + 1, :] * extended[first : first + STRETCH]
    conv = (running * jax.nn.sigmoid(running)).astype(jnp.bfloat16)
    conv_ref[0] = conv

    @pl.when(pl.program_id(1) == 0)
    def _():
        b_mat[...] = conv[:, :N]

    @pl.when(pl.program_id(1) > 0)
    def _():
        lane = lax.broadcasted_iota(jnp.int32, (STRETCH, N), 1)
        for pair in range(HEADS // 2):
            tails = jnp.where(
                lane < N // 2,
                tail_ref[0, 0, :, 2 * pair : 2 * pair + 1],
                tail_ref[0, 0, :, 2 * pair + 1 : 2 * pair + 2],
            )
            weighted = (conv[:, pair * N : (pair + 1) * N].astype(jnp.float32) * tails).astype(
                jnp.bfloat16
            )
            state_ref[0, pair * N : (pair + 1) * N, :] = lax.dot_general(
                weighted, b_mat[...], (((0,), (0,)), ((), ())), preferred_element_type=jnp.float32
            ).astype(jnp.bfloat16)


def mix_kernel(x_ref, bc_ref, col_ref, row_ref, state_ref, skip_ref, y_ref, scores):
    half = STRETCH // 2

    @pl.when(pl.program_id(1) == 0)
    def _():
        scores[...] = lax.dot_general(
            bc_ref[0, :, N:], bc_ref[0, :, :N], (((1,), (1,)), ((), ())),
            preferred_element_type=jnp.float32,
        )

    lane = lax.broadcasted_iota(jnp.int32, (half, N), 1)
    low = lane < N // 2
    causal = lax.broadcasted_iota(jnp.int32, (half, half), 0) >= lax.broadcasted_iota(
        jnp.int32, (half, half), 1
    )
    c_mat = bc_ref[0, :, N:]
    for pair in range(HEADS // 2):
        lanes = slice(pair * N, (pair + 1) * N)
        x_pair = x_ref[0, :, lanes]
        y_off = lax.dot_general(
            c_mat, state_ref[0, lanes, :], (((1,), (1,)), ((), ())),
            preferred_element_type=jnp.float32,
        )
        tops, bottoms = [], []
        for head in (2 * pair, 2 * pair + 1):
            col = col_ref[0, 0, :, head : head + 1]
            row = row_ref[0, 0, head : head + 1, :]
            top = jnp.exp2(jnp.where(causal, col[:half] - row[:, :half], -1e30))
            top = (top * scores[:half, :half]).astype(jnp.bfloat16)
            tops.append(jnp.dot(top, x_pair[:half], preferred_element_type=jnp.float32))
            left = jnp.exp2(col[half:] - row[:, :half])
            left = (left * scores[half:, :half]).astype(jnp.bfloat16)
            right = jnp.exp2(jnp.where(causal, col[half:] - row[:, half:], -1e30))
            right = (right * scores[half:, half:]).astype(jnp.bfloat16)
            bottoms.append(
                jnp.dot(
                    jnp.concatenate([left, right], axis=1), x_pair,
                    preferred_element_type=jnp.float32,
                )
            )
        skip = skip_ref[:, lanes]
        for part, (first, second) in enumerate((tops, bottoms)):
            rows = slice(part * half, (part + 1) * half)
            decay = jnp.exp2(
                jnp.where(
                    low,
                    col_ref[0, 0, rows, 2 * pair : 2 * pair + 1],
                    col_ref[0, 0, rows, 2 * pair + 1 : 2 * pair + 2],
                )
            )
            y = jnp.where(low, first, second) + decay * y_off[rows]
            y = y + skip * x_pair[rows].astype(jnp.float32)
            y_ref[0, rows, lanes] = y.astype(jnp.bfloat16)


def conv_and_state(rows, history, weight, bias, tails, inner):
    blocks = inner // WIDTH
    channels = weight.shape[1]

    def column(block):
        return jnp.where(block == 0, blocks, block - 1)

    def earlier(block):
        return jnp.maximum(block - 1, 0)

    return pl.pallas_call(
        conv_kernel,
        grid=(2, blocks + 1),
        in_specs=[
            pl.BlockSpec((1, STRETCH, WIDTH), lambda i, b: (i, 0, column(b))),
            pl.BlockSpec((1, HIST, WIDTH), lambda i, b: (i, 0, column(b))),
            pl.BlockSpec((weight.shape[0], WIDTH), lambda i, b: (0, column(b))),
            pl.BlockSpec((1, WIDTH), lambda i, b: (0, column(b))),
            pl.BlockSpec((1, 1, STRETCH, HEADS), lambda i, b: (i, earlier(b), 0, 0)),
        ],
        out_specs=[
            pl.BlockSpec((1, STRETCH, WIDTH), lambda i, b: (i, 0, column(b))),
            pl.BlockSpec((1, WIDTH, N), lambda i, b: (i, earlier(b), 0)),
        ],
        out_shape=[
            jax.ShapeDtypeStruct((2, STRETCH, channels), jnp.bfloat16),
            jax.ShapeDtypeStruct((2, inner, N), jnp.bfloat16),
        ],
        scratch_shapes=[pltpu.VMEM((STRETCH, N), jnp.bfloat16)],
        name="conv_and_state",
    )(rows, history, weight, bias, tails)


def mix(conv, col, row, state_in, skip, inner):
    blocks = inner // WIDTH
    return pl.pallas_call(
        mix_kernel,
        grid=(2, blocks),
        in_specs=[
            pl.BlockSpec((1, STRETCH, WIDTH), lambda i, b: (i, 0, b)),
            pl.BlockSpec((1, STRETCH, WIDTH), lambda i, b: (i, 0, blocks)),
            pl.BlockSpec((1, 1, STRETCH, HEADS), lambda i, b: (i, b, 0, 0)),
            pl.BlockSpec((1, 1, HEADS, STRETCH), lambda i, b: (i, b, 0, 0)),
            pl.BlockSpec((1, WIDTH, N), lambda i, b: (i, b, 0)),
            pl.BlockSpec((1, WIDTH), lambda i, b: (0, b)),
        ],
        out_specs=pl.BlockSpec((1, STRETCH, WIDTH), lambda i, b: (i, 0, b)),
        out_shape=jax.ShapeDtypeStruct((2, STRETCH, inner), jnp.bfloat16),
        scratch_shapes=[pltpu.VMEM((STRETCH, STRETCH), jnp.float32)],
        name="mix",
    )(conv, conv, col, row, state_in, skip)


def per_device(
    x_in,
    bc_in,
    z_in,
    dt_raw,
    conv_weight,
    conv_bias,
    dt_bias,
    a_log,
    d_skip,
    norm_gain,
    w_out,
    prompt_stretches,
):
    n_req, n_seq = lax.axis_size("req"), lax.axis_size("seq")
    group = n_req // 2
    tokens, inner = x_in.shape
    heads = a_log.shape[0]
    head_dim = inner // heads
    span = conv_weight.shape[0]
    part = tokens // n_req
    req, seq = lax.axis_index("req"), lax.axis_index("seq")
    half, place = req // group, req % group
    same_half = [[h * group + q for q in range(group)] for h in range(2)]

    lengths = prompt_stretches
    firsts = jnp.cumsum(lengths) - lengths
    stretch_total = n_req * n_seq * 2
    every = jnp.arange(stretch_total, dtype=jnp.int32)
    all_starts = jnp.any(every[:, None] == firsts[None, :], axis=1)
    all_finals = jnp.any(every[:, None] == (firsts + lengths - 1)[None, :], axis=1)

    def gather_stretches(rows):
        cut = rows.reshape(2, group, part, rows.shape[-1])
        return lax.all_to_all(
            cut, "req", split_axis=1, concat_axis=1, tiled=True, axis_index_groups=same_half
        )

    packed = jnp.concatenate([x_in, bc_in, dt_raw], axis=1)
    rows = gather_stretches(packed).reshape(2, STRETCH, packed.shape[1])
    channels = inner + 2 * N

    def index_of(h, q, s):
        return (h * group + q) * n_seq + s

    moves = [[], []]
    for q in range(group):
        for s in range(n_seq):
            for slot in range(2):
                moves[slot].append((index_of(0, q, s), index_of(1, q, s)))
                if s + 1 < n_seq:
                    moves[slot].append((index_of(1, q, s), index_of(0, q, s + 1)))
        source = index_of(1, q, n_seq - 1)
        if q + 1 < group:
            for slot in range(2):
                moves[slot].append((source, index_of(0, q + 1, 0)))
        else:
            moves[0].append((source, index_of(0, 0, 0)))
    ends = rows[:, STRETCH - (span - 1) :, :channels]
    got = [lax.ppermute(ends[slot], ("req", "seq"), moves[slot]) for slot in range(2)]
    wrapped = (req == 0) & (seq == 0)
    own = (jnp.arange(2) * group + place) * (2 * n_seq) + 2 * seq + half
    history = jnp.stack(
        [jnp.where(wrapped, got[1], got[0]), jnp.where(wrapped, got[0], got[1])]
    )
    own_starts = all_starts[own]
    history = jnp.where(own_starts[:, None, None], jnp.zeros_like(history), history)
    history = jnp.pad(history, ((0, 0), (HIST - (span - 1), 0), (0, 0)))

    step = jax.nn.softplus(rows[:, :, channels:].astype(jnp.float32) + dt_bias)
    triangle = jnp.tril(jnp.ones((STRETCH, STRETCH), jnp.float32))
    log_decay = jnp.einsum(
        "tu,cuh->cth", triangle, -jnp.exp(a_log) * step, precision=lax.Precision.HIGHEST
    )
    last = log_decay[:, -1, :]
    tails = jnp.exp(last[:, None, :] - log_decay) * step

    def by_block(value):
        return value.reshape(2, STRETCH, heads // HEADS, HEADS)

    col = by_block(log_decay * LOG2E).transpose(0, 2, 1, 3)
    row = by_block(log_decay * LOG2E - jnp.log2(step)).transpose(0, 2, 3, 1)
    tails = by_block(tails).transpose(0, 2, 1, 3)

    gains = lax.all_gather(jnp.exp(last), ("req", "seq"), axis=0)
    gains = gains.reshape(2, group, n_seq, 2, heads).transpose(3, 1, 2, 0, 4)
    gains = gains.reshape(stretch_total, heads)
    heads_here = heads // n_seq
    gains = lax.dynamic_slice_in_dim(gains, seq * heads_here, heads_here, axis=1)
    gains = jnp.where(all_starts[:, None], 0.0, gains)

    conv, states = conv_and_state(rows, history, conv_weight, conv_bias[None, :], tails, inner)

    pairs = [
        [index_of(h, q, s) for h in range(2) for s in range(n_seq)] for q in range(group)
    ]

    def by_heads(value):
        value = value.reshape(2 * n_seq, heads_here * head_dim, N)
        return lax.all_to_all(
            value, ("req", "seq"), split_axis=0, concat_axis=0, tiled=True, axis_index_groups=pairs
        )

    held = by_heads(states).reshape(2, n_seq, heads_here, head_dim, N).astype(jnp.float32)
    held_count = 2 * n_seq
    first_held = req * held_count

    def gain_of(stretch):
        return gains[stretch][:, None, None]

    total = jnp.zeros((heads_here, head_dim, N), jnp.float32)
    for k in range(held_count):
        total = gain_of(first_held + k) * total + held[k % 2, k // 2]
    total = total.astype(jnp.bfloat16)
    reach = min(-(-(LMAX_CH - 1) // held_count), n_req - 1)
    incoming = jnp.zeros_like(total, jnp.float32)
    reach_gain = jnp.ones((heads_here,), jnp.float32)
    for steps in range(1, reach + 1):
        arrived = lax.ppermute(total, "req", [(i, i + steps) for i in range(n_req - steps)])
        incoming = incoming + reach_gain[:, None, None] * arrived.astype(jnp.float32)
        before = jnp.maximum(req - steps, 0) * held_count
        reach_gain = reach_gain * jnp.prod(
            lax.dynamic_slice_in_dim(gains, before, held_count, axis=0), axis=0
        )
    entering = [[None] * n_seq, [None] * n_seq]
    endings = []
    previous = incoming
    for k in range(held_count):
        start = all_starts[first_held + k]
        entering[k % 2][k // 2] = jnp.where(start, 0.0, previous).astype(jnp.bfloat16)
        previous = gain_of(first_held + k) * previous + held[k % 2, k // 2]
        endings.append(jnp.where(all_finals[first_held + k], previous, 0.0))
    endings = jnp.stack(endings)
    state_in = by_heads(jnp.stack(entering[0] + entering[1])).reshape(2, inner, N)

    skip = jnp.repeat(d_skip, head_dim)[None, :]
    y = mix(conv, col, row, state_in, skip, inner)
    y = gather_stretches(y.reshape(tokens, inner)).reshape(tokens, inner).astype(jnp.float32)
    gated = y * jax.nn.silu(z_in.astype(jnp.float32))
    inv_rms = lax.rsqrt(jnp.mean(gated * gated, axis=-1, keepdims=True) + 1e-05)
    normed = (gated * inv_rms * norm_gain[None, :]).astype(jnp.bfloat16)
    mixed_out = jnp.dot(normed, w_out, preferred_element_type=jnp.float32).astype(jnp.bfloat16)
    return (mixed_out, endings)


def solution(mesh):
    rows = P(("req", "seq"), None)
    return jax.shard_map(
        per_device,
        mesh=mesh,
        in_specs=(rows,) * 4 + (P(),) * 8,
        out_specs=(rows, P("req", "seq", None, None)),
        check_vma=False,
    )
```

```python
import math

import jax
import jax.numpy as jnp
from jax import lax
from jax.experimental import pallas as pl
from jax.experimental.pallas import tpu as pltpu
from jax.sharding import PartitionSpec as P

N = 128
STRETCH = 256
LMAX_CH = 16
HIST = 8
GAIN_ROWS = 16
VMEM = 40 * 1024 * 1024
LOG2E = math.log2(math.e)


def silu_conv(extended, weight_ref, bias_ref):
    span = weight_ref.shape[0]
    running = bias_ref[...]
    for offset in range(span):
        first = HIST - (span - 1) + offset
        running = running + weight_ref[offset : offset + 1, :] * extended[first : first + STRETCH]
    return (running * jax.nn.sigmoid(running)).astype(jnp.bfloat16)


def conv_kernel(
    rows_ref, hist_ref, weight_ref, bias_ref,
    bc_rows_ref, bc_hist_ref, bc_weight_ref, bc_bias_ref,
    tail_ref, gain_ref, conv_ref, bc_ref, state_ref,
):
    @pl.when(pl.program_id(1) == 0)
    def _():
        extended = jnp.concatenate(
            [bc_hist_ref[0].astype(jnp.float32), bc_rows_ref[0].astype(jnp.float32)], axis=0
        )
        bc_ref[0] = silu_conv(extended, bc_weight_ref, bc_bias_ref)

    extended = jnp.concatenate(
        [hist_ref[0].astype(jnp.float32), rows_ref[0].astype(jnp.float32)], axis=0
    )
    conv = silu_conv(extended, weight_ref, bias_ref)
    conv_ref[0] = conv
    b_mat = bc_ref[0, :, :N]
    lane = lax.broadcasted_iota(jnp.int32, (STRETCH, N), 1)
    width = conv.shape[1]
    for pair in range(width // N):
        tails = jnp.where(
            lane < N // 2,
            tail_ref[0, 0, :, 2 * pair : 2 * pair + 1],
            tail_ref[0, 0, :, 2 * pair + 1 : 2 * pair + 2],
        )
        weighted = (conv[:, pair * N : (pair + 1) * N].astype(jnp.float32) * tails).astype(
            jnp.bfloat16
        )
        state_ref[0, 0, pair * N : (pair + 1) * N, :] = lax.dot_general(
            weighted, b_mat, (((0,), (0,)), ((), ())), preferred_element_type=jnp.float32
        ).astype(jnp.bfloat16)
    state_ref[0, 0, width:, :] = gain_ref[0, 0]


def mix_kernel(x_ref, bc_ref, col_ref, row_ref, skip_ref, y_ref, scores):
    half = STRETCH // 2

    @pl.when(pl.program_id(1) == 0)
    def _():
        scores[...] = lax.dot_general(
            bc_ref[0, :, N:], bc_ref[0, :, :N], (((1,), (1,)), ((), ())),
            preferred_element_type=jnp.float32,
        )

    lane = lax.broadcasted_iota(jnp.int32, (half, N), 1)
    low = lane < N // 2
    causal = lax.broadcasted_iota(jnp.int32, (half, half), 0) >= lax.broadcasted_iota(
        jnp.int32, (half, half), 1
    )
    for pair in range(x_ref.shape[2] // N):
        lanes = slice(pair * N, (pair + 1) * N)
        x_pair = x_ref[0, :, lanes]
        tops, bottoms = [], []
        for head in (2 * pair, 2 * pair + 1):
            col = col_ref[0, 0, :, head : head + 1]
            row = row_ref[0, 0, head : head + 1, :]
            top = jnp.exp2(jnp.where(causal, col[:half] - row[:, :half], -1e30))
            top = (top * scores[:half, :half]).astype(jnp.bfloat16)
            tops.append(jnp.dot(top, x_pair[:half], preferred_element_type=jnp.float32))
            left = jnp.exp2(col[half:] - row[:, :half])
            left = (left * scores[half:, :half]).astype(jnp.bfloat16)
            right = jnp.exp2(jnp.where(causal, col[half:] - row[:, half:], -1e30))
            right = (right * scores[half:, half:]).astype(jnp.bfloat16)
            bottoms.append(
                jnp.dot(
                    jnp.concatenate([left, right], axis=1), x_pair,
                    preferred_element_type=jnp.float32,
                )
            )
        skip = skip_ref[:, lanes]
        for part, (first, second) in enumerate((tops, bottoms)):
            rows = slice(part * half, (part + 1) * half)
            y = jnp.where(low, first, second) + skip * x_pair[rows].astype(jnp.float32)
            y_ref[0, rows, lanes] = y


def carry_kernel(diag_ref, bc_ref, col_ref, state_ref, y_ref):
    c_mat = bc_ref[0, :, N:]
    low = lax.broadcasted_iota(jnp.int32, (STRETCH, N), 1) < N // 2
    for pair in range(diag_ref.shape[2] // N):
        lanes = slice(pair * N, (pair + 1) * N)
        y_off = lax.dot_general(
            c_mat, state_ref[0, 0, lanes, :], (((1,), (1,)), ((), ())),
            preferred_element_type=jnp.float32,
        )
        decay = jnp.exp2(
            jnp.where(
                low,
                col_ref[0, 0, :, 2 * pair : 2 * pair + 1],
                col_ref[0, 0, :, 2 * pair + 1 : 2 * pair + 2],
            )
        )
        y_ref[0, :, lanes] = (diag_ref[0, :, lanes] + decay * y_off).astype(jnp.bfloat16)


def gain_row(ref, index, rows):
    pieces = ref[index, rows : rows + GAIN_ROWS, :].astype(jnp.float32)
    return pieces[0:1] + pieces[1:2] + pieces[2:3]


def held_index(stretch, count):
    return (stretch % 2) * (count // 2) + stretch // 2


def total_kernel(starts_ref, held_ref, total_ref):
    count, rows = held_ref.shape[0], held_ref.shape[1] - GAIN_ROWS
    dim = N // 2
    gains = []
    for k in range(count):
        gain = gain_row(held_ref, held_index(k, count), rows)
        gains.append(jnp.where(starts_ref[k] > 0, 0.0, gain))
    product = gains[0]
    for k in range(1, count):
        product = product * gains[k]
    for head in range(rows // dim):
        span = slice(head * dim, (head + 1) * dim)
        total = held_ref[0, span, :].astype(jnp.float32)
        for k in range(1, count):
            total = gains[k][:, head : head + 1] * total + held_ref[
                held_index(k, count), span, :
            ].astype(jnp.float32)
        total_ref[span, :] = total.astype(jnp.bfloat16)
    high = product.astype(jnp.bfloat16).astype(jnp.float32)
    middle = (product - high).astype(jnp.bfloat16).astype(jnp.float32)
    rest = product - high - middle
    place = lax.broadcasted_iota(jnp.int32, (GAIN_ROWS, N), 0)
    total_ref[rows:, :] = jnp.where(
        place == 0, high, jnp.where(place == 1, middle, jnp.where(place == 2, rest, 0.0))
    ).astype(jnp.bfloat16)


def scan_kernel(starts_ref, finals_ref, held_ref, arrived_ref, state_ref, ending_ref):
    count, rows = held_ref.shape[0], held_ref.shape[1] - GAIN_ROWS
    dim = N // 2
    gains = [gain_row(held_ref, held_index(k, count), rows) for k in range(count)]
    reach = arrived_ref.shape[0]
    farther = [gain_row(arrived_ref, steps, rows) for steps in range(reach)]
    for head in range(rows // dim):
        span = slice(head * dim, (head + 1) * dim)
        state = arrived_ref[reach - 1, span, :].astype(jnp.float32)
        for steps in range(reach - 2, -1, -1):
            state = farther[steps][:, head : head + 1] * state + arrived_ref[
                steps, span, :
            ].astype(jnp.float32)
        for k in range(count):
            here = held_index(k, count)
            state = jnp.where(starts_ref[k] > 0, 0.0, state)
            state_ref[here, span, :] = state.astype(jnp.bfloat16)
            state = gains[k][:, head : head + 1] * state + held_ref[here, span, :].astype(
                jnp.float32
            )
            ending_ref[k, span, :] = jnp.where(finals_ref[k] > 0, state, 0.0)


def conv_and_state(rows, history, weight, bias, tails, gain_rows, inner):
    blocks = tails.shape[1]
    width = inner // blocks
    pair = 2 * N
    bc = inner // pair
    span = weight.shape[0]
    return pl.pallas_call(
        conv_kernel,
        grid=(2, blocks),
        in_specs=[
            pl.BlockSpec((1, STRETCH, width), lambda i, b: (i, 0, b)),
            pl.BlockSpec((1, HIST, width), lambda i, b: (i, 0, b)),
            pl.BlockSpec((span, width), lambda i, b: (0, b)),
            pl.BlockSpec((1, width), lambda i, b: (0, b)),
            pl.BlockSpec((1, STRETCH, pair), lambda i, b: (i, 0, bc)),
            pl.BlockSpec((1, HIST, pair), lambda i, b: (i, 0, bc)),
            pl.BlockSpec((span, pair), lambda i, b: (0, bc)),
            pl.BlockSpec((1, pair), lambda i, b: (0, bc)),
            pl.BlockSpec((1, 1) + tails.shape[2:], lambda i, b: (i, b, 0, 0)),
            pl.BlockSpec((1, 1, GAIN_ROWS, N), lambda i, b: (i, b, 0, 0)),
        ],
        out_specs=[
            pl.BlockSpec((1, STRETCH, width), lambda i, b: (i, 0, b)),
            pl.BlockSpec((1, STRETCH, pair), lambda i, b: (i, 0, 0)),
            pl.BlockSpec((1, 1, width + GAIN_ROWS, N), lambda i, b: (i, b, 0, 0)),
        ],
        out_shape=[
            jax.ShapeDtypeStruct((2, STRETCH, inner), jnp.bfloat16),
            jax.ShapeDtypeStruct((2, STRETCH, pair), jnp.bfloat16),
            jax.ShapeDtypeStruct((2, blocks, width + GAIN_ROWS, N), jnp.bfloat16),
        ],
        compiler_params=pltpu.CompilerParams(vmem_limit_bytes=VMEM),
        name="conv_and_state",
    )(rows, history, weight, bias, rows, history, weight, bias, tails, gain_rows)


def mix(conv, bc, col, row, skip):
    blocks = col.shape[1]
    width = conv.shape[2] // blocks
    return pl.pallas_call(
        mix_kernel,
        grid=(2, blocks),
        in_specs=[
            pl.BlockSpec((1, STRETCH, width), lambda i, b: (i, 0, b)),
            pl.BlockSpec((1, STRETCH, 2 * N), lambda i, b: (i, 0, 0)),
            pl.BlockSpec((1, 1) + col.shape[2:], lambda i, b: (i, b, 0, 0)),
            pl.BlockSpec((1, 1) + row.shape[2:], lambda i, b: (i, b, 0, 0)),
            pl.BlockSpec((1, width), lambda i, b: (0, b)),
        ],
        out_specs=pl.BlockSpec((1, STRETCH, width), lambda i, b: (i, 0, b)),
        out_shape=jax.ShapeDtypeStruct(conv.shape, jnp.float32),
        scratch_shapes=[pltpu.VMEM((STRETCH, STRETCH), jnp.float32)],
        compiler_params=pltpu.CompilerParams(vmem_limit_bytes=VMEM),
        cost_estimate=pl.CostEstimate(
            flops=15_000_000_000, bytes_accessed=8_000_000, transcendentals=5_000_000
        ),
        name="mix",
    )(conv, bc, col, row, skip)


def add_carried(diag, bc, col, state_in):
    blocks = col.shape[1]
    width = diag.shape[2] // blocks
    return pl.pallas_call(
        carry_kernel,
        grid=(2, blocks),
        in_specs=[
            pl.BlockSpec((1, STRETCH, width), lambda i, b: (i, 0, b)),
            pl.BlockSpec((1, STRETCH, 2 * N), lambda i, b: (i, 0, 0)),
            pl.BlockSpec((1, 1) + col.shape[2:], lambda i, b: (i, b, 0, 0)),
            pl.BlockSpec((1, 1, width, N), lambda i, b: (i, b, 0, 0)),
        ],
        out_specs=pl.BlockSpec((1, STRETCH, width), lambda i, b: (i, 0, b)),
        out_shape=jax.ShapeDtypeStruct(diag.shape, jnp.bfloat16),
        compiler_params=pltpu.CompilerParams(vmem_limit_bytes=VMEM),
        name="add_carried",
    )(diag, bc, col, state_in)


def held_total(starts, held):
    return pl.pallas_call(
        total_kernel,
        in_specs=[
            pl.BlockSpec(memory_space=pltpu.SMEM),
            pl.BlockSpec(memory_space=pltpu.VMEM),
        ],
        out_specs=pl.BlockSpec(memory_space=pltpu.VMEM),
        out_shape=jax.ShapeDtypeStruct(held.shape[1:], jnp.bfloat16),
        compiler_params=pltpu.CompilerParams(vmem_limit_bytes=VMEM),
        name="held_total",
    )(starts, held)


def held_scan(starts, finals, held, arrived):
    rows = held.shape[1] - GAIN_ROWS
    return pl.pallas_call(
        scan_kernel,
        in_specs=[pl.BlockSpec(memory_space=pltpu.SMEM)] * 2
        + [pl.BlockSpec(memory_space=pltpu.VMEM)] * 2,
        out_specs=[pl.BlockSpec(memory_space=pltpu.VMEM)] * 2,
        out_shape=[
            jax.ShapeDtypeStruct((held.shape[0], rows, N), jnp.bfloat16),
            jax.ShapeDtypeStruct((held.shape[0], rows, N), jnp.float32),
        ],
        compiler_params=pltpu.CompilerParams(vmem_limit_bytes=VMEM),
        name="held_scan",
    )(starts, finals, held, arrived)


def per_device(
    x_in,
    bc_in,
    z_in,
    dt_raw,
    conv_weight,
    conv_bias,
    dt_bias,
    a_log,
    d_skip,
    norm_gain,
    w_out,
    prompt_stretches,
):
    n_req, n_seq = lax.axis_size("req"), lax.axis_size("seq")
    group = n_req // 2
    tokens, inner = x_in.shape
    heads = a_log.shape[0]
    head_dim = inner // heads
    span = conv_weight.shape[0]
    part = tokens // n_req
    req, seq = lax.axis_index("req"), lax.axis_index("seq")
    half, place = req // group, req % group
    same_half = [[h * group + q for q in range(group)] for h in range(2)]

    lengths = prompt_stretches
    firsts = jnp.cumsum(lengths) - lengths
    stretch_total = n_req * n_seq * 2
    every = jnp.arange(stretch_total, dtype=jnp.int32)
    all_starts = jnp.any(every[:, None] == firsts[None, :], axis=1)
    all_finals = jnp.any(every[:, None] == (firsts + lengths - 1)[None, :], axis=1)

    def gather_stretches(rows):
        cut = rows.reshape(2, group, part, rows.shape[-1])
        return lax.all_to_all(
            cut, "req", split_axis=1, concat_axis=1, tiled=True, axis_index_groups=same_half
        )

    packed = jnp.concatenate([x_in, bc_in, dt_raw], axis=1)
    rows = gather_stretches(packed).reshape(2, STRETCH, packed.shape[1])
    channels = inner + 2 * N

    def index_of(h, q, s):
        return (h * group + q) * n_seq + s

    moves = []
    for q in range(group):
        for s in range(n_seq):
            moves.append((index_of(0, q, s), index_of(1, q, s)))
            following = index_of(0, q, s + 1) if s + 1 < n_seq else index_of(0, (q + 1) % group, 0)
            moves.append((index_of(1, q, s), following))
    got = lax.ppermute(rows[:, STRETCH - (span - 1) :, :channels], ("req", "seq"), moves)
    wrapped = (req == 0) & (seq == 0)
    history = jnp.where(wrapped, jnp.stack([jnp.zeros_like(got[0]), got[0]]), got)
    own = (jnp.arange(2) * group + place) * (2 * n_seq) + 2 * seq + half
    own_starts = all_starts[own]
    history = jnp.where(own_starts[:, None, None], jnp.zeros_like(history), history)
    history = jnp.pad(history, ((0, 0), (HIST - (span - 1), 0), (0, 0)))

    step = jax.nn.softplus(rows[:, :, channels:].astype(jnp.float32) + dt_bias)
    triangle = jnp.tril(jnp.ones((STRETCH, STRETCH), jnp.float32))
    log_decay = jnp.einsum(
        "tu,cuh->cth", triangle, -jnp.exp(a_log) * step, precision=lax.Precision.HIGHEST
    )
    last = log_decay[:, -1, :]
    tails = jnp.exp(last[:, None, :] - log_decay) * step

    heads_here = heads // n_seq

    def by_block(value):
        return value.reshape(2, STRETCH, n_seq, heads_here)

    col = by_block(log_decay * LOG2E).transpose(0, 2, 1, 3)
    row = by_block(log_decay * LOG2E - jnp.log2(step)).transpose(0, 2, 3, 1)
    tails = by_block(tails).transpose(0, 2, 1, 3)
    gain = jnp.exp(last).reshape(2, n_seq, 1, heads_here)
    high = lax.reduce_precision(gain, 8, 7)
    middle = lax.reduce_precision(gain - high, 8, 7)
    gain_rows = jnp.concatenate([high, middle, gain - high - middle], axis=2).astype(jnp.bfloat16)
    gain_rows = jnp.pad(gain_rows, ((0, 0), (0, 0), (0, GAIN_ROWS - 3), (0, N - heads_here)))

    conv, conv_bc, states = conv_and_state(
        rows, history, conv_weight, conv_bias[None, :], tails, gain_rows, inner
    )
    skip = jnp.repeat(d_skip, head_dim)[None, :]
    diag = mix(conv, conv_bc, col, row, skip)

    pairs = [
        [index_of(h, q, s) for h in range(2) for s in range(n_seq)] for q in range(group)
    ]

    def by_heads(value):
        return lax.all_to_all(
            value, ("req", "seq"), split_axis=0, concat_axis=0, tiled=True, axis_index_groups=pairs
        )

    held_count = 2 * n_seq
    held = by_heads(states.reshape(held_count, states.shape[2], N))
    held_starts = lax.dynamic_slice_in_dim(all_starts, req * held_count, held_count)
    held_finals = lax.dynamic_slice_in_dim(all_finals, req * held_count, held_count)
    held_starts = held_starts.astype(jnp.int32)
    total = held_total(held_starts, held)
    reach = min(-(-(LMAX_CH - 1) // held_count), n_req - 1)
    arrived = jnp.stack(
        [
            lax.ppermute(total, "req", [(i, i + steps) for i in range(n_req - steps)])
            for steps in range(1, reach + 1)
        ]
    )
    state_in, endings = held_scan(held_starts, held_finals.astype(jnp.int32), held, arrived)
    endings = endings.reshape(held_count, heads_here, head_dim, N)
    state_in = by_heads(state_in).reshape(2, n_seq, heads_here * head_dim, N)
    y = add_carried(diag, conv_bc, col, state_in)
    y = gather_stretches(y.reshape(tokens, inner)).reshape(tokens, inner).astype(jnp.float32)
    gated = y * jax.nn.silu(z_in.astype(jnp.float32))
    inv_rms = lax.rsqrt(jnp.mean(gated * gated, axis=-1, keepdims=True) + 1e-05)
    normed = (gated * inv_rms * norm_gain[None, :]).astype(jnp.bfloat16)
    mixed_out = jnp.dot(normed, w_out, preferred_element_type=jnp.float32).astype(jnp.bfloat16)
    return (mixed_out, endings)


def solution(mesh):
    rows = P(("req", "seq"), None)
    return jax.shard_map(
        per_device,
        mesh=mesh,
        in_specs=(rows,) * 4 + (P(),) * 8,
        out_specs=(rows, P("req", "seq", None, None)),
        check_vma=False,
    )
```

```python
import math

import jax
import jax.numpy as jnp
from jax import lax
from jax.experimental import pallas as pl
from jax.experimental.pallas import tpu as pltpu
from jax.sharding import PartitionSpec as P

N = 128
STRETCH = 256
LMAX_CH = 16
HIST = 8
GAIN_ROWS = 16
VMEM = 40 * 1024 * 1024
LOG2E = math.log2(math.e)


def silu_conv(extended, weight_ref, bias_ref):
    span = weight_ref.shape[0]
    running = bias_ref[...]
    for offset in range(span):
        first = HIST - (span - 1) + offset
        running = running + weight_ref[offset : offset + 1, :] * extended[first : first + STRETCH]
    return (running * jax.nn.sigmoid(running)).astype(jnp.bfloat16)


def conv_kernel(*refs):
    rows_ref, hist_ref, weight_ref, bias_ref, tail_ref, gain_ref = refs[:6]
    if len(refs) == 9:
        bc_ref, conv_ref, state_ref = refs[6:]
    else:
        bc_rows_ref, bc_hist_ref, bc_weight_ref, bc_bias_ref, conv_ref, state_ref, bc_ref = refs[6:]

        @pl.when(pl.program_id(1) == 0)
        def _():
            extended = jnp.concatenate(
                [bc_hist_ref[0].astype(jnp.float32), bc_rows_ref[0].astype(jnp.float32)], axis=0
            )
            bc_ref[0] = silu_conv(extended, bc_weight_ref, bc_bias_ref)

    extended = jnp.concatenate(
        [hist_ref[0].astype(jnp.float32), rows_ref[0].astype(jnp.float32)], axis=0
    )
    conv = silu_conv(extended, weight_ref, bias_ref)
    conv_ref[0] = conv
    b_mat = bc_ref[0, :, :N]
    lane = lax.broadcasted_iota(jnp.int32, (STRETCH, N), 1)
    width = conv.shape[1]
    for pair in range(width // N):
        tails = jnp.where(
            lane < N // 2,
            tail_ref[0, 0, :, 2 * pair : 2 * pair + 1],
            tail_ref[0, 0, :, 2 * pair + 1 : 2 * pair + 2],
        )
        weighted = (conv[:, pair * N : (pair + 1) * N].astype(jnp.float32) * tails).astype(
            jnp.bfloat16
        )
        state_ref[0, 0, pair * N : (pair + 1) * N, :] = lax.dot_general(
            weighted, b_mat, (((0,), (0,)), ((), ())), preferred_element_type=jnp.float32
        ).astype(jnp.bfloat16)
    state_ref[0, 0, width:, :] = gain_ref[0, 0]


def mix_kernel(x_ref, bc_ref, col_ref, row_ref, skip_ref, y_ref, scores):
    half = STRETCH // 2

    @pl.when(pl.program_id(1) == 0)
    def _():
        scores[...] = lax.dot_general(
            bc_ref[0, :, N:], bc_ref[0, :, :N], (((1,), (1,)), ((), ())),
            preferred_element_type=jnp.float32,
        )

    lane = lax.broadcasted_iota(jnp.int32, (half, N), 1)
    low = lane < N // 2
    causal = lax.broadcasted_iota(jnp.int32, (half, half), 0) >= lax.broadcasted_iota(
        jnp.int32, (half, half), 1
    )
    for pair in range(x_ref.shape[2] // N):
        lanes = slice(pair * N, (pair + 1) * N)
        x_pair = x_ref[0, :, lanes]
        tops, bottoms = [], []
        for head in (2 * pair, 2 * pair + 1):
            col = col_ref[0, 0, :, head : head + 1]
            row = row_ref[0, 0, head : head + 1, :]
            top = jnp.exp2(jnp.where(causal, col[:half] - row[:, :half], -1e30))
            top = (top * scores[:half, :half]).astype(jnp.bfloat16)
            tops.append(jnp.dot(top, x_pair[:half], preferred_element_type=jnp.float32))
            left = jnp.exp2(col[half:] - row[:, :half])
            left = (left * scores[half:, :half]).astype(jnp.bfloat16)
            right = jnp.exp2(jnp.where(causal, col[half:] - row[:, half:], -1e30))
            right = (right * scores[half:, half:]).astype(jnp.bfloat16)
            bottoms.append(
                jnp.dot(
                    jnp.concatenate([left, right], axis=1), x_pair,
                    preferred_element_type=jnp.float32,
                )
            )
        skip = skip_ref[:, lanes]
        for part, (first, second) in enumerate((tops, bottoms)):
            rows = slice(part * half, (part + 1) * half)
            y = jnp.where(low, first, second) + skip * x_pair[rows].astype(jnp.float32)
            y_ref[0, rows, lanes] = y


def carry_kernel(diag_ref, bc_ref, col_ref, state_ref, y_ref):
    c_mat = bc_ref[0, :, N:]
    low = lax.broadcasted_iota(jnp.int32, (STRETCH, N), 1) < N // 2
    for pair in range(diag_ref.shape[2] // N):
        lanes = slice(pair * N, (pair + 1) * N)
        y_off = lax.dot_general(
            c_mat, state_ref[0, 0, lanes, :], (((1,), (1,)), ((), ())),
            preferred_element_type=jnp.float32,
        )
        decay = jnp.exp2(
            jnp.where(
                low,
                col_ref[0, 0, :, 2 * pair : 2 * pair + 1],
                col_ref[0, 0, :, 2 * pair + 1 : 2 * pair + 2],
            )
        )
        y_ref[0, :, lanes] = (diag_ref[0, :, lanes] + decay * y_off).astype(jnp.bfloat16)


def gain_row(ref, index, rows):
    pieces = ref[index, rows : rows + GAIN_ROWS, :].astype(jnp.float32)
    return pieces[0:1] + pieces[1:2] + pieces[2:3]


def held_index(stretch, count):
    return (stretch % 2) * (count // 2) + stretch // 2


def total_kernel(starts_ref, held_ref, total_ref):
    count, rows = held_ref.shape[0], held_ref.shape[1] - GAIN_ROWS
    dim = N // 2
    gains = []
    for k in range(count):
        gain = gain_row(held_ref, held_index(k, count), rows)
        gains.append(jnp.where(starts_ref[k] > 0, 0.0, gain))
    product = gains[0]
    for k in range(1, count):
        product = product * gains[k]
    for head in range(rows // dim):
        span = slice(head * dim, (head + 1) * dim)
        total = held_ref[0, span, :].astype(jnp.float32)
        for k in range(1, count):
            total = gains[k][:, head : head + 1] * total + held_ref[
                held_index(k, count), span, :
            ].astype(jnp.float32)
        total_ref[span, :] = total.astype(jnp.bfloat16)
    high = product.astype(jnp.bfloat16).astype(jnp.float32)
    middle = (product - high).astype(jnp.bfloat16).astype(jnp.float32)
    rest = product - high - middle
    place = lax.broadcasted_iota(jnp.int32, (GAIN_ROWS, N), 0)
    total_ref[rows:, :] = jnp.where(
        place == 0, high, jnp.where(place == 1, middle, jnp.where(place == 2, rest, 0.0))
    ).astype(jnp.bfloat16)


def scan_kernel(starts_ref, finals_ref, held_ref, arrived_ref, state_ref, ending_ref):
    count, rows = held_ref.shape[0], held_ref.shape[1] - GAIN_ROWS
    dim = N // 2
    gains = [gain_row(held_ref, held_index(k, count), rows) for k in range(count)]
    reach = arrived_ref.shape[0]
    farther = [gain_row(arrived_ref, steps, rows) for steps in range(reach)]
    for head in range(rows // dim):
        span = slice(head * dim, (head + 1) * dim)
        state = arrived_ref[reach - 1, span, :].astype(jnp.float32)
        for steps in range(reach - 2, -1, -1):
            state = farther[steps][:, head : head + 1] * state + arrived_ref[
                steps, span, :
            ].astype(jnp.float32)
        for k in range(count):
            here = held_index(k, count)
            state = jnp.where(starts_ref[k] > 0, 0.0, state)
            state_ref[here, span, :] = state.astype(jnp.bfloat16)
            state = gains[k][:, head : head + 1] * state + held_ref[here, span, :].astype(
                jnp.float32
            )
            ending_ref[k, span, :] = jnp.where(finals_ref[k] > 0, state, 0.0)


def conv_and_state(rows, history, weight, bias, tails, gain_rows, inner, conv_bc):
    blocks = tails.shape[1]
    width = inner // blocks
    pair = 2 * N
    bc = inner // pair
    span = weight.shape[0]
    in_specs = [
        pl.BlockSpec((1, STRETCH, width), lambda i, b: (i, 0, b)),
        pl.BlockSpec((1, HIST, width), lambda i, b: (i, 0, b)),
        pl.BlockSpec((span, width), lambda i, b: (0, b)),
        pl.BlockSpec((1, width), lambda i, b: (0, b)),
        pl.BlockSpec((1, 1) + tails.shape[2:], lambda i, b: (i, b, 0, 0)),
        pl.BlockSpec((1, 1, GAIN_ROWS, N), lambda i, b: (i, b, 0, 0)),
    ]
    out_specs = [
        pl.BlockSpec((1, STRETCH, width), lambda i, b: (i, 0, b)),
        pl.BlockSpec((1, 1, width + GAIN_ROWS, N), lambda i, b: (i, b, 0, 0)),
    ]
    out_shape = [
        jax.ShapeDtypeStruct((2, STRETCH, inner), jnp.bfloat16),
        jax.ShapeDtypeStruct((2, blocks, width + GAIN_ROWS, N), jnp.bfloat16),
    ]
    args = [rows, history, weight, bias, tails, gain_rows]
    bc_spec = pl.BlockSpec((1, STRETCH, pair), lambda i, b: (i, 0, 0))
    if conv_bc is None:
        in_specs += [
            pl.BlockSpec((1, STRETCH, pair), lambda i, b: (i, 0, bc)),
            pl.BlockSpec((1, HIST, pair), lambda i, b: (i, 0, bc)),
            pl.BlockSpec((span, pair), lambda i, b: (0, bc)),
            pl.BlockSpec((1, pair), lambda i, b: (0, bc)),
        ]
        args += [rows, history, weight, bias]
        out_specs.append(bc_spec)
        out_shape.append(jax.ShapeDtypeStruct((2, STRETCH, pair), jnp.bfloat16))
    else:
        in_specs.append(bc_spec)
        args.append(conv_bc)
    made = pl.pallas_call(
        conv_kernel,
        grid=(2, blocks),
        in_specs=in_specs,
        out_specs=out_specs,
        out_shape=out_shape,
        compiler_params=pltpu.CompilerParams(vmem_limit_bytes=VMEM),
        cost_estimate=pl.CostEstimate(
            flops=6_000_000_000, bytes_accessed=5_000_000, transcendentals=1_000_000
        ),
        name="conv_and_state",
    )(*args)
    return made if conv_bc is None else (*made, conv_bc)


def mix(conv, bc, col, row, skip):
    blocks = col.shape[1]
    width = conv.shape[2] // blocks
    return pl.pallas_call(
        mix_kernel,
        grid=(2, blocks),
        in_specs=[
            pl.BlockSpec((1, STRETCH, width), lambda i, b: (i, 0, b)),
            pl.BlockSpec((1, STRETCH, 2 * N), lambda i, b: (i, 0, 0)),
            pl.BlockSpec((1, 1) + col.shape[2:], lambda i, b: (i, b, 0, 0)),
            pl.BlockSpec((1, 1) + row.shape[2:], lambda i, b: (i, b, 0, 0)),
            pl.BlockSpec((1, width), lambda i, b: (0, b)),
        ],
        out_specs=pl.BlockSpec((1, STRETCH, width), lambda i, b: (i, 0, b)),
        out_shape=jax.ShapeDtypeStruct(conv.shape, jnp.float32),
        scratch_shapes=[pltpu.VMEM((STRETCH, STRETCH), jnp.float32)],
        compiler_params=pltpu.CompilerParams(vmem_limit_bytes=VMEM),
        cost_estimate=pl.CostEstimate(
            flops=4_000_000_000, bytes_accessed=4_000_000, transcendentals=2_000_000
        ),
        name="mix",
    )(conv, bc, col, row, skip)


def add_carried(diag, bc, col, state_in):
    blocks = col.shape[1]
    width = diag.shape[2] // blocks
    return pl.pallas_call(
        carry_kernel,
        grid=(2, blocks),
        in_specs=[
            pl.BlockSpec((1, STRETCH, width), lambda i, b: (i, 0, b)),
            pl.BlockSpec((1, STRETCH, 2 * N), lambda i, b: (i, 0, 0)),
            pl.BlockSpec((1, 1) + col.shape[2:], lambda i, b: (i, b, 0, 0)),
            pl.BlockSpec((1, 1, width, N), lambda i, b: (i, b, 0, 0)),
        ],
        out_specs=pl.BlockSpec((1, STRETCH, width), lambda i, b: (i, 0, b)),
        out_shape=jax.ShapeDtypeStruct(diag.shape, jnp.bfloat16),
        compiler_params=pltpu.CompilerParams(vmem_limit_bytes=VMEM),
        name="add_carried",
    )(diag, bc, col, state_in)


def held_total(starts, held):
    return pl.pallas_call(
        total_kernel,
        in_specs=[
            pl.BlockSpec(memory_space=pltpu.SMEM),
            pl.BlockSpec(memory_space=pltpu.VMEM),
        ],
        out_specs=pl.BlockSpec(memory_space=pltpu.VMEM),
        out_shape=jax.ShapeDtypeStruct(held.shape[1:], jnp.bfloat16),
        compiler_params=pltpu.CompilerParams(vmem_limit_bytes=VMEM),
        name="held_total",
    )(starts, held)


def held_scan(starts, finals, held, arrived):
    rows = held.shape[1] - GAIN_ROWS
    return pl.pallas_call(
        scan_kernel,
        in_specs=[pl.BlockSpec(memory_space=pltpu.SMEM)] * 2
        + [pl.BlockSpec(memory_space=pltpu.VMEM)] * 2,
        out_specs=[pl.BlockSpec(memory_space=pltpu.VMEM)] * 2,
        out_shape=[
            jax.ShapeDtypeStruct((held.shape[0], rows, N), jnp.bfloat16),
            jax.ShapeDtypeStruct((held.shape[0], rows, N), jnp.float32),
        ],
        compiler_params=pltpu.CompilerParams(vmem_limit_bytes=VMEM),
        name="held_scan",
    )(starts, finals, held, arrived)


def per_device(
    x_in,
    bc_in,
    z_in,
    dt_raw,
    conv_weight,
    conv_bias,
    dt_bias,
    a_log,
    d_skip,
    norm_gain,
    w_out,
    prompt_stretches,
):
    n_req, n_seq = lax.axis_size("req"), lax.axis_size("seq")
    group = n_req // 2
    tokens, inner = x_in.shape
    heads = a_log.shape[0]
    head_dim = inner // heads
    span = conv_weight.shape[0]
    part = tokens // n_req
    req, seq = lax.axis_index("req"), lax.axis_index("seq")
    half, place = req // group, req % group
    same_half = [[h * group + q for q in range(group)] for h in range(2)]

    lengths = prompt_stretches
    firsts = jnp.cumsum(lengths) - lengths
    stretch_total = n_req * n_seq * 2
    every = jnp.arange(stretch_total, dtype=jnp.int32)
    all_starts = jnp.any(every[:, None] == firsts[None, :], axis=1)
    all_finals = jnp.any(every[:, None] == (firsts + lengths - 1)[None, :], axis=1)

    def gather_stretches(rows):
        cut = rows.reshape(2, group, part, rows.shape[-1])
        return lax.all_to_all(
            cut, "req", split_axis=1, concat_axis=1, tiled=True, axis_index_groups=same_half
        )

    heads_here = heads // n_seq
    chunk = inner // n_seq
    cut = 2 * (heads_here // 4 + 1)
    parts = [(0, cut), (cut, heads_here)]

    def columns(value, first, end, base=0):
        return [
            value[..., base + s * chunk + first * head_dim : base + s * chunk + end * head_dim]
            for s in range(n_seq)
        ]

    packed = jnp.concatenate(columns(x_in, *parts[0]) + [bc_in, dt_raw], axis=1)
    rows = gather_stretches(packed).reshape(2, STRETCH, packed.shape[1])
    second = jnp.concatenate(columns(x_in, *parts[1]), axis=1)
    second, _ = lax.optimization_barrier((second, rows))
    second_rows = gather_stretches(second).reshape(2, STRETCH, second.shape[1])
    width = cut * head_dim * n_seq
    channels = width + 2 * N

    def index_of(h, q, s):
        return (h * group + q) * n_seq + s

    moves = []
    for q in range(group):
        for s in range(n_seq):
            moves.append((index_of(0, q, s), index_of(1, q, s)))
            following = index_of(0, q, s + 1) if s + 1 < n_seq else index_of(0, (q + 1) % group, 0)
            moves.append((index_of(1, q, s), following))
    own = (jnp.arange(2) * group + place) * (2 * n_seq) + 2 * seq + half
    own_starts = all_starts[own]
    wrapped = (req == 0) & (seq == 0)

    def history_of(ends):
        got = lax.ppermute(ends, ("req", "seq"), moves)
        history = jnp.where(wrapped, jnp.stack([jnp.zeros_like(got[0]), got[0]]), got)
        history = jnp.where(own_starts[:, None, None], jnp.zeros_like(history), history)
        return jnp.pad(history, ((0, 0), (HIST - (span - 1), 0), (0, 0)))

    histories = [
        history_of(rows[:, STRETCH - (span - 1) :, :channels]),
        history_of(second_rows[:, STRETCH - (span - 1) :, :]),
    ]

    step = jax.nn.softplus(rows[:, :, channels:].astype(jnp.float32) + dt_bias)
    triangle = jnp.tril(jnp.ones((STRETCH, STRETCH), jnp.float32))
    log_decay = jnp.einsum(
        "tu,cuh->cth", triangle, -jnp.exp(a_log) * step, precision=lax.Precision.HIGHEST
    )
    last = log_decay[:, -1, :]
    tails = jnp.exp(last[:, None, :] - log_decay) * step

    def by_block(value):
        return value.reshape(2, STRETCH, n_seq, heads_here)

    col = by_block(log_decay * LOG2E).transpose(0, 2, 1, 3)
    row = by_block(log_decay * LOG2E - jnp.log2(step)).transpose(0, 2, 3, 1)
    tails = by_block(tails).transpose(0, 2, 1, 3)
    gain = jnp.exp(last).reshape(2, n_seq, 1, heads_here)
    high = lax.reduce_precision(gain, 8, 7)
    middle = lax.reduce_precision(gain - high, 8, 7)
    gain_rows = jnp.concatenate([high, middle, gain - high - middle], axis=2).astype(jnp.bfloat16)
    skip = jnp.repeat(d_skip, head_dim)[None, :]

    pairs = [
        [index_of(h, q, s) for h in range(2) for s in range(n_seq)] for q in range(group)
    ]

    def by_heads(value):
        return lax.all_to_all(
            value, ("req", "seq"), split_axis=0, concat_axis=0, tiled=True, axis_index_groups=pairs
        )

    held_count = 2 * n_seq
    held_starts = lax.dynamic_slice_in_dim(all_starts, req * held_count, held_count)
    held_finals = lax.dynamic_slice_in_dim(all_finals, req * held_count, held_count)
    held_starts = held_starts.astype(jnp.int32)
    held_finals = held_finals.astype(jnp.int32)
    reach = min(-(-(LMAX_CH - 1) // held_count), n_req - 1)
    conv_bc = None
    y_parts, ending_parts = [], []
    for index, (first, end) in enumerate(parts):
        count = end - first
        inner_part = count * head_dim * n_seq
        tail_columns = [conv_weight[:, inner:]] if index == 0 else []
        weight = jnp.concatenate(columns(conv_weight, first, end) + tail_columns, axis=1)
        tail_columns = [conv_bias[inner:]] if index == 0 else []
        bias = jnp.concatenate(columns(conv_bias, first, end) + tail_columns)[None, :]
        gain_part = jnp.pad(
            gain_rows[..., first:end], ((0, 0), (0, 0), (0, GAIN_ROWS - 3), (0, N - count))
        )
        conv, states, conv_bc = conv_and_state(
            (rows, second_rows)[index], histories[index], weight, bias,
            tails[..., first:end], gain_part, inner_part, conv_bc,
        )
        col_part = col[..., first:end]
        skip_part = jnp.concatenate(columns(skip, first, end), axis=1)
        diag = mix(conv, conv_bc, col_part, row[:, :, first:end, :], skip_part)
        held = by_heads(states.reshape(held_count, states.shape[2], N))
        total = held_total(held_starts, held)
        arrived = jnp.stack(
            [
                lax.ppermute(total, "req", [(i, i + steps) for i in range(n_req - steps)])
                for steps in range(1, reach + 1)
            ]
        )
        state_in, endings = held_scan(held_starts, held_finals, held, arrived)
        ending_parts.append(endings.reshape(held_count, count, head_dim, N))
        state_in = by_heads(state_in).reshape(2, n_seq, count * head_dim, N)
        y = add_carried(diag, conv_bc, col_part, state_in)
        y_parts.append(gather_stretches(y.reshape(tokens, inner_part)).reshape(tokens, inner_part))
    endings = jnp.concatenate(ending_parts, axis=1)
    pieces = []
    for s in range(n_seq):
        for (first, end), y in zip(parts, y_parts):
            size = (end - first) * head_dim
            pieces.append(y[:, s * size : (s + 1) * size])
    y = jnp.concatenate(pieces, axis=1).astype(jnp.float32)
    gated = y * jax.nn.silu(z_in.astype(jnp.float32))
    inv_rms = lax.rsqrt(jnp.mean(gated * gated, axis=-1, keepdims=True) + 1e-05)
    normed = (gated * inv_rms * norm_gain[None, :]).astype(jnp.bfloat16)
    mixed_out = jnp.dot(normed, w_out, preferred_element_type=jnp.float32).astype(jnp.bfloat16)
    return (mixed_out, endings)


def solution(mesh):
    rows = P(("req", "seq"), None)
    return jax.shard_map(
        per_device,
        mesh=mesh,
        in_specs=(rows,) * 4 + (P(),) * 8,
        out_specs=(rows, P("req", "seq", None, None)),
        check_vma=False,
    )
```

```python
import math

import jax
import jax.numpy as jnp
from jax import lax
from jax.experimental import pallas as pl
from jax.experimental.pallas import tpu as pltpu
from jax.sharding import PartitionSpec as P

N = 128
STRETCH = 256
LMAX_CH = 16
HIST = 8
GAIN_ROWS = 16
VMEM = 60 * 1024 * 1024
LOG2E = math.log2(math.e)


def silu_conv(extended, weight_ref, bias_ref):
    span = weight_ref.shape[0]
    running = bias_ref[...]
    for offset in range(span):
        first = HIST - (span - 1) + offset
        running = running + weight_ref[offset : offset + 1, :] * extended[first : first + STRETCH]
    return (running * jax.nn.sigmoid(running)).astype(jnp.bfloat16)


def conv_kernel(
    rows_ref, hist_ref, weight_ref, bias_ref,
    bc_rows_ref, bc_hist_ref, bc_weight_ref, bc_bias_ref,
    tail_ref, gain_ref, conv_ref, bc_ref, state_ref,
):
    @pl.when(pl.program_id(1) == 0)
    def _():
        extended = jnp.concatenate(
            [bc_hist_ref[0].astype(jnp.float32), bc_rows_ref[0].astype(jnp.float32)], axis=0
        )
        bc_ref[0] = silu_conv(extended, bc_weight_ref, bc_bias_ref)

    extended = jnp.concatenate(
        [hist_ref[0].astype(jnp.float32), rows_ref[0].astype(jnp.float32)], axis=0
    )
    conv = silu_conv(extended, weight_ref, bias_ref)
    conv_ref[0] = conv
    b_mat = bc_ref[0, :, :N]
    lane = lax.broadcasted_iota(jnp.int32, (STRETCH, N), 1)
    width = conv.shape[1]
    for pair in range(width // N):
        tails = jnp.where(
            lane < N // 2,
            tail_ref[0, 0, :, 2 * pair : 2 * pair + 1],
            tail_ref[0, 0, :, 2 * pair + 1 : 2 * pair + 2],
        )
        weighted = (conv[:, pair * N : (pair + 1) * N].astype(jnp.float32) * tails).astype(
            jnp.bfloat16
        )
        state_ref[0, 0, pair * N : (pair + 1) * N, :] = lax.dot_general(
            weighted, b_mat, (((0,), (0,)), ((), ())), preferred_element_type=jnp.float32
        ).astype(jnp.bfloat16)
    state_ref[0, 0, width:, :] = gain_ref[0, 0]


def mix_kernel(x_ref, bc_ref, col_ref, row_ref, skip_ref, y_ref, scores):
    half = STRETCH // 2

    @pl.when(pl.program_id(1) == 0)
    def _():
        scores[...] = lax.dot_general(
            bc_ref[0, :, N:], bc_ref[0, :, :N], (((1,), (1,)), ((), ())),
            preferred_element_type=jnp.float32,
        )

    lane = lax.broadcasted_iota(jnp.int32, (half, N), 1)
    low = lane < N // 2
    causal = lax.broadcasted_iota(jnp.int32, (half, half), 0) >= lax.broadcasted_iota(
        jnp.int32, (half, half), 1
    )
    for pair in range(x_ref.shape[2] // N):
        lanes = slice(pair * N, (pair + 1) * N)
        x_pair = x_ref[0, :, lanes]
        tops, bottoms = [], []
        for head in (2 * pair, 2 * pair + 1):
            col = col_ref[0, 0, :, head : head + 1]
            row = row_ref[0, 0, head : head + 1, :]
            top = jnp.exp2(jnp.where(causal, col[:half] - row[:, :half], -1e30))
            top = (top * scores[:half, :half]).astype(jnp.bfloat16)
            tops.append(jnp.dot(top, x_pair[:half], preferred_element_type=jnp.float32))
            left = jnp.exp2(col[half:] - row[:, :half])
            left = (left * scores[half:, :half]).astype(jnp.bfloat16)
            right = jnp.exp2(jnp.where(causal, col[half:] - row[:, half:], -1e30))
            right = (right * scores[half:, half:]).astype(jnp.bfloat16)
            bottoms.append(
                jnp.dot(
                    jnp.concatenate([left, right], axis=1), x_pair,
                    preferred_element_type=jnp.float32,
                )
            )
        skip = skip_ref[:, lanes]
        for part, (first, second) in enumerate((tops, bottoms)):
            rows = slice(part * half, (part + 1) * half)
            y = jnp.where(low, first, second) + skip * x_pair[rows].astype(jnp.float32)
            y_ref[0, rows, lanes] = y


def carry_kernel(diag_ref, bc_ref, col_ref, state_ref, y_ref):
    c_mat = bc_ref[0, :, N:]
    low = lax.broadcasted_iota(jnp.int32, (STRETCH, N), 1) < N // 2
    for pair in range(diag_ref.shape[2] // N):
        lanes = slice(pair * N, (pair + 1) * N)
        y_off = lax.dot_general(
            c_mat, state_ref[0, 0, lanes, :], (((1,), (1,)), ((), ())),
            preferred_element_type=jnp.float32,
        )
        decay = jnp.exp2(
            jnp.where(
                low,
                col_ref[0, 0, :, 2 * pair : 2 * pair + 1],
                col_ref[0, 0, :, 2 * pair + 1 : 2 * pair + 2],
            )
        )
        y_ref[0, :, lanes] = (diag_ref[0, :, lanes] + decay * y_off).astype(jnp.bfloat16)


def gain_row(ref, index, rows):
    pieces = ref[index, rows : rows + GAIN_ROWS, :].astype(jnp.float32)
    return pieces[0:1] + pieces[1:2] + pieces[2:3]


def held_index(stretch, count):
    return (stretch % 2) * (count // 2) + stretch // 2


def total_kernel(starts_ref, held_ref, total_ref):
    count, rows = held_ref.shape[0], held_ref.shape[1] - GAIN_ROWS
    dim = N // 2
    gains = []
    for k in range(count):
        gain = gain_row(held_ref, held_index(k, count), rows)
        gains.append(jnp.where(starts_ref[k] > 0, 0.0, gain))
    product = gains[0]
    for k in range(1, count):
        product = product * gains[k]
    for head in range(rows // dim):
        span = slice(head * dim, (head + 1) * dim)
        total = held_ref[0, span, :].astype(jnp.float32)
        for k in range(1, count):
            total = gains[k][:, head : head + 1] * total + held_ref[
                held_index(k, count), span, :
            ].astype(jnp.float32)
        total_ref[span, :] = total.astype(jnp.bfloat16)
    high = product.astype(jnp.bfloat16).astype(jnp.float32)
    middle = (product - high).astype(jnp.bfloat16).astype(jnp.float32)
    rest = product - high - middle
    place = lax.broadcasted_iota(jnp.int32, (GAIN_ROWS, N), 0)
    total_ref[rows:, :] = jnp.where(
        place == 0, high, jnp.where(place == 1, middle, jnp.where(place == 2, rest, 0.0))
    ).astype(jnp.bfloat16)


def scan_kernel(starts_ref, finals_ref, held_ref, arrived_ref, state_ref, ending_ref):
    count, rows = held_ref.shape[0], held_ref.shape[1] - GAIN_ROWS
    dim = N // 2
    gains = [gain_row(held_ref, held_index(k, count), rows) for k in range(count)]
    reach = arrived_ref.shape[0]
    farther = [gain_row(arrived_ref, steps, rows) for steps in range(reach)]
    for head in range(rows // dim):
        span = slice(head * dim, (head + 1) * dim)
        state = arrived_ref[reach - 1, span, :].astype(jnp.float32)
        for steps in range(reach - 2, -1, -1):
            state = farther[steps][:, head : head + 1] * state + arrived_ref[
                steps, span, :
            ].astype(jnp.float32)
        for k in range(count):
            here = held_index(k, count)
            state = jnp.where(starts_ref[k] > 0, 0.0, state)
            state_ref[here, span, :] = state.astype(jnp.bfloat16)
            state = gains[k][:, head : head + 1] * state + held_ref[here, span, :].astype(
                jnp.float32
            )
            ending_ref[k, span, :] = jnp.where(finals_ref[k] > 0, state, 0.0)


def conv_and_state(rows, history, weight, bias, tails, gain_rows, inner):
    blocks = tails.shape[1]
    width = inner // blocks
    pair = 2 * N
    bc = inner // pair
    span = weight.shape[0]
    return pl.pallas_call(
        conv_kernel,
        grid=(2, blocks),
        in_specs=[
            pl.BlockSpec((1, STRETCH, width), lambda i, b: (i, 0, b)),
            pl.BlockSpec((1, HIST, width), lambda i, b: (i, 0, b)),
            pl.BlockSpec((span, width), lambda i, b: (0, b)),
            pl.BlockSpec((1, width), lambda i, b: (0, b)),
            pl.BlockSpec((1, STRETCH, pair), lambda i, b: (i, 0, bc)),
            pl.BlockSpec((1, HIST, pair), lambda i, b: (i, 0, bc)),
            pl.BlockSpec((span, pair), lambda i, b: (0, bc)),
            pl.BlockSpec((1, pair), lambda i, b: (0, bc)),
            pl.BlockSpec((1, 1) + tails.shape[2:], lambda i, b: (i, b, 0, 0)),
            pl.BlockSpec((1, 1, GAIN_ROWS, N), lambda i, b: (i, b, 0, 0)),
        ],
        out_specs=[
            pl.BlockSpec((1, STRETCH, width), lambda i, b: (i, 0, b)),
            pl.BlockSpec((1, STRETCH, pair), lambda i, b: (i, 0, 0)),
            pl.BlockSpec((1, 1, width + GAIN_ROWS, N), lambda i, b: (i, b, 0, 0)),
        ],
        out_shape=[
            jax.ShapeDtypeStruct((2, STRETCH, inner), jnp.bfloat16),
            jax.ShapeDtypeStruct((2, STRETCH, pair), jnp.bfloat16),
            jax.ShapeDtypeStruct((2, blocks, width + GAIN_ROWS, N), jnp.bfloat16),
        ],
        compiler_params=pltpu.CompilerParams(vmem_limit_bytes=VMEM),
        name="conv_and_state",
    )(rows, history, weight, bias, rows, history, weight, bias, tails, gain_rows)


def mix(conv, bc, col, row, skip):
    blocks = col.shape[1]
    width = conv.shape[2] // blocks
    return pl.pallas_call(
        mix_kernel,
        grid=(2, blocks),
        in_specs=[
            pl.BlockSpec((1, STRETCH, width), lambda i, b: (i, 0, b)),
            pl.BlockSpec((1, STRETCH, 2 * N), lambda i, b: (i, 0, 0)),
            pl.BlockSpec((1, 1) + col.shape[2:], lambda i, b: (i, b, 0, 0)),
            pl.BlockSpec((1, 1) + row.shape[2:], lambda i, b: (i, b, 0, 0)),
            pl.BlockSpec((1, width), lambda i, b: (0, b)),
        ],
        out_specs=pl.BlockSpec((1, STRETCH, width), lambda i, b: (i, 0, b)),
        out_shape=jax.ShapeDtypeStruct(conv.shape, jnp.float32),
        scratch_shapes=[pltpu.VMEM((STRETCH, STRETCH), jnp.float32)],
        compiler_params=pltpu.CompilerParams(vmem_limit_bytes=VMEM),
        cost_estimate=pl.CostEstimate(
            flops=15_000_000_000, bytes_accessed=8_000_000, transcendentals=5_000_000
        ),
        name="mix",
    )(conv, bc, col, row, skip)


def add_carried(diag, bc, col, state_in):
    blocks = col.shape[1]
    width = diag.shape[2] // blocks
    return pl.pallas_call(
        carry_kernel,
        grid=(2, blocks),
        in_specs=[
            pl.BlockSpec((1, STRETCH, width), lambda i, b: (i, 0, b)),
            pl.BlockSpec((1, STRETCH, 2 * N), lambda i, b: (i, 0, 0)),
            pl.BlockSpec((1, 1) + col.shape[2:], lambda i, b: (i, b, 0, 0)),
            pl.BlockSpec((1, 1, width, N), lambda i, b: (i, b, 0, 0)),
        ],
        out_specs=pl.BlockSpec((1, STRETCH, width), lambda i, b: (i, 0, b)),
        out_shape=jax.ShapeDtypeStruct(diag.shape, jnp.bfloat16),
        compiler_params=pltpu.CompilerParams(vmem_limit_bytes=VMEM),
        name="add_carried",
    )(diag, bc, col, state_in)


def held_total(starts, held):
    return pl.pallas_call(
        total_kernel,
        in_specs=[
            pl.BlockSpec(memory_space=pltpu.SMEM),
            pl.BlockSpec(memory_space=pltpu.VMEM),
        ],
        out_specs=pl.BlockSpec(memory_space=pltpu.VMEM),
        out_shape=jax.ShapeDtypeStruct(held.shape[1:], jnp.bfloat16),
        compiler_params=pltpu.CompilerParams(vmem_limit_bytes=VMEM),
        name="held_total",
    )(starts, held)


def held_scan(starts, finals, held, arrived):
    rows = held.shape[1] - GAIN_ROWS
    return pl.pallas_call(
        scan_kernel,
        in_specs=[pl.BlockSpec(memory_space=pltpu.SMEM)] * 2
        + [pl.BlockSpec(memory_space=pltpu.VMEM)] * 2,
        out_specs=[pl.BlockSpec(memory_space=pltpu.VMEM)] * 2,
        out_shape=[
            jax.ShapeDtypeStruct((held.shape[0], rows, N), jnp.bfloat16),
            jax.ShapeDtypeStruct((held.shape[0], rows, N), jnp.float32),
        ],
        compiler_params=pltpu.CompilerParams(vmem_limit_bytes=VMEM),
        name="held_scan",
    )(starts, finals, held, arrived)


def per_device(
    x_in,
    bc_in,
    z_in,
    dt_raw,
    conv_weight,
    conv_bias,
    dt_bias,
    a_log,
    d_skip,
    norm_gain,
    w_out,
    prompt_stretches,
):
    n_req, n_seq = lax.axis_size("req"), lax.axis_size("seq")
    group = n_req // 2
    tokens, inner = x_in.shape
    heads = a_log.shape[0]
    head_dim = inner // heads
    span = conv_weight.shape[0]
    part = tokens // n_req
    req, seq = lax.axis_index("req"), lax.axis_index("seq")
    half, place = req // group, req % group
    same_half = [[h * group + q for q in range(group)] for h in range(2)]

    lengths = prompt_stretches
    firsts = jnp.cumsum(lengths) - lengths
    stretch_total = n_req * n_seq * 2
    every = jnp.arange(stretch_total, dtype=jnp.int32)
    all_starts = jnp.any(every[:, None] == firsts[None, :], axis=1)
    all_finals = jnp.any(every[:, None] == (firsts + lengths - 1)[None, :], axis=1)

    def gather_stretches(rows):
        cut = rows.reshape(2, group, part, rows.shape[-1])
        return lax.all_to_all(
            cut, "req", split_axis=1, concat_axis=1, tiled=True, axis_index_groups=same_half
        )

    packed = jnp.concatenate([x_in, bc_in, dt_raw], axis=1)
    rows = gather_stretches(packed).reshape(2, STRETCH, packed.shape[1])
    channels = inner + 2 * N

    def index_of(h, q, s):
        return (h * group + q) * n_seq + s

    moves = []
    for q in range(group):
        for s in range(n_seq):
            moves.append((index_of(0, q, s), index_of(1, q, s)))
            following = index_of(0, q, s + 1) if s + 1 < n_seq else index_of(0, (q + 1) % group, 0)
            moves.append((index_of(1, q, s), following))
    got = lax.ppermute(rows[:, STRETCH - (span - 1) :, :channels], ("req", "seq"), moves)
    wrapped = (req == 0) & (seq == 0)
    history = jnp.where(wrapped, jnp.stack([jnp.zeros_like(got[0]), got[0]]), got)
    own = (jnp.arange(2) * group + place) * (2 * n_seq) + 2 * seq + half
    own_starts = all_starts[own]
    history = jnp.where(own_starts[:, None, None], jnp.zeros_like(history), history)
    history = jnp.pad(history, ((0, 0), (HIST - (span - 1), 0), (0, 0)))

    step = jax.nn.softplus(rows[:, :, channels:].astype(jnp.float32) + dt_bias)
    triangle = jnp.tril(jnp.ones((STRETCH, STRETCH), jnp.float32))
    log_decay = jnp.einsum(
        "tu,cuh->cth", triangle, -jnp.exp(a_log) * step, precision=lax.Precision.HIGHEST
    )
    last = log_decay[:, -1, :]
    tails = jnp.exp(last[:, None, :] - log_decay) * step

    heads_here = heads // n_seq

    def by_block(value):
        return value.reshape(2, STRETCH, n_seq, heads_here)

    col = by_block(log_decay * LOG2E).transpose(0, 2, 1, 3)
    row = by_block(log_decay * LOG2E - jnp.log2(step)).transpose(0, 2, 3, 1)
    tails = by_block(tails).transpose(0, 2, 1, 3)
    gain = jnp.exp(last).reshape(2, n_seq, 1, heads_here)
    high = lax.reduce_precision(gain, 8, 7)
    middle = lax.reduce_precision(gain - high, 8, 7)
    gain_rows = jnp.concatenate([high, middle, gain - high - middle], axis=2).astype(jnp.bfloat16)
    gain_rows = jnp.pad(gain_rows, ((0, 0), (0, 0), (0, GAIN_ROWS - 3), (0, N - heads_here)))

    conv, conv_bc, states = conv_and_state(
        rows, history, conv_weight, conv_bias[None, :], tails, gain_rows, inner
    )
    skip = jnp.repeat(d_skip, head_dim)[None, :]
    diag = mix(conv, conv_bc, col, row, skip)

    pairs = [
        [index_of(h, q, s) for h in range(2) for s in range(n_seq)] for q in range(group)
    ]

    def by_heads(value):
        return lax.all_to_all(
            value, ("req", "seq"), split_axis=0, concat_axis=0, tiled=True, axis_index_groups=pairs
        )

    held_count = 2 * n_seq
    held = by_heads(states.reshape(held_count, states.shape[2], N))
    held_starts = lax.dynamic_slice_in_dim(all_starts, req * held_count, held_count)
    held_finals = lax.dynamic_slice_in_dim(all_finals, req * held_count, held_count)
    held_starts = held_starts.astype(jnp.int32)
    total = held_total(held_starts, held)
    reach = min(-(-(LMAX_CH - 1) // held_count), n_req - 1)
    arrived = jnp.stack(
        [
            lax.ppermute(total, "req", [(i, i + steps) for i in range(n_req - steps)])
            for steps in range(1, reach + 1)
        ]
    )
    state_in, endings = held_scan(held_starts, held_finals.astype(jnp.int32), held, arrived)
    endings = endings.reshape(held_count, heads_here, head_dim, N)
    state_in = by_heads(state_in).reshape(2, n_seq, heads_here * head_dim, N)
    y = add_carried(diag, conv_bc, col, state_in)
    y = gather_stretches(y.reshape(tokens, inner)).reshape(tokens, inner).astype(jnp.float32)
    gated = y * jax.nn.silu(z_in.astype(jnp.float32))
    inv_rms = lax.rsqrt(jnp.mean(gated * gated, axis=-1, keepdims=True) + 1e-05)
    normed = (gated * inv_rms * norm_gain[None, :]).astype(jnp.bfloat16)
    mixed_out = jnp.dot(normed, w_out, preferred_element_type=jnp.float32).astype(jnp.bfloat16)
    return (mixed_out, endings)


def solution(mesh):
    rows = P(("req", "seq"), None)
    return jax.shard_map(
        per_device,
        mesh=mesh,
        in_specs=(rows,) * 4 + (P(),) * 8,
        out_specs=(rows, P("req", "seq", None, None)),
        check_vma=False,
    )
```
